32 devices in a mesh: groups: 2 (over x), gz: 8 (over z, y), gy: 2 (over core).
Axes of the slice: x: 2, y: 2, z: 4, core: 2. Of those that a mesh axis runs over, the one named last changes fastest.
Arguments:
- momentum: float32 [3, 64, 64, 1024], P(None, ('groups', 'gz'), 'gy'), parts along dimension 1, may hold values from -4 to 4
- template: float32 [64, 64, 1024], P(('groups', 'gz'), 'gy'), parts along dimension 0, may hold values from -6 to 6
- target: float32 [64, 64, 1024], P(('groups', 'gz'), 'gy'), parts along dimension 0, may hold values from -6 to 6
Outputs:
- momentum_out: float32 [3, 64, 64, 1024], P(None, ('groups', 'gz'), 'gy'), parts along dimension 1
- deformed: float32 [64, 64, 1024], P(('groups', 'gz'), 'gy'), parts along dimension 0
- gradient: float32 [3, 64, 64, 1024], P(None, ('groups', 'gz'), 'gy'), parts along dimension 1
The draws below stay inside these ranges and needn't reach their ends.
There are 2 independent parts, one for each index of `groups`. The reference program is written for one: setup_inputs(seed, part) draws one part's arguments, and reference() takes and returns one part's arrays. A program takes and returns all parts, laid end to end along the dimension named above; each array names one. Nothing has to cross between parts.
All inputs are finite; a program needn't handle non-finite values.
Results may differ from the reference program's by a relative error of at most 0.00002.
Values sent between devices are 32-bit elements; how exact they have to be, the bound alone decides.
A program may use at most 64 MiB of HBM per device.

```python
import jax
import jax.numpy as jnp
from jax import lax

NX = 1024
STEPS = 2
NZ = 32
NY = 64


def block_scale(key, extent, pieces, low, high):
    def one(position, blocks):
        heights = jax.random.uniform(jax.random.fold_in(jax.random.fold_in(key, 6), position), (blocks,), jnp.float32, low / len(pieces), high / len(pieces))
        return jnp.repeat(jnp.exp(heights), extent[position] // blocks).reshape((-1,) + (1,) * (len(extent) - position - 1))

    loudness = one(*pieces[0])
    for cut in pieces[1:]:
        loudness = loudness * one(*cut)
    return loudness


def centred(stream_key, dims, spread, bound, shards=(), held_as=jnp.bfloat16):
    gain = block_scale(stream_key, dims, shards, -0.22, 0.18) if shards else 1.0
    values = jax.random.normal(stream_key, dims, jnp.float32) * spread * gain
    return jnp.minimum(jnp.maximum(values, -bound), bound).astype(held_as)


def setup_inputs(seed: int = 0, part: int = 0) -> dict:
    seeds = jax.random.split(jax.random.key(seed), 4)
    part_keys = jax.random.split(jax.random.fold_in(seeds[3], part), 4)
    return {
        "momentum": centred(part_keys[0], (3, NZ, NY, NX), 1.0, 4.0, ((1, 8), (2, 2)), jnp.float32),
        "template": centred(part_keys[1], (NZ, NY, NX), 1.0, 6.0, ((0, 8), (1, 2)), jnp.float32),
        "target": centred(part_keys[2], (NZ, NY, NX), 1.0, 6.0, ((0, 8), (1, 2)), jnp.float32),
    }


TAPS = (0.05, 0.1, 0.2, 0.3, 0.2, 0.1, 0.05)
STEP_SIZE = 0.25


def taps_sum(padded, axis, length):
    total = jnp.zeros(padded.shape[:axis] + (length,) + padded.shape[axis + 1:], jnp.float32)
    for k in range(7):
        total = total + TAPS[k] * lax.slice_in_dim(padded, k, k + length, axis=axis)
    return total


def pad_axis(field, axis, width):
    widths = [(0, 0)] * field.ndim
    widths[axis] = (width, width)
    return jnp.pad(field, widths)


def smooth(field):
    for axis in (3, 2, 1):
        field = taps_sum(pad_axis(field, axis, 3), axis, field.shape[axis])
    return field


def pad_one(field):
    return jnp.pad(field, ((0, 0), (1, 1), (1, 1), (1, 1)))


def window(padded, axis, offset):
    out = padded
    for ax in (1, 2, 3):
        start = 1 + (offset if ax == axis else 0)
        out = lax.slice_in_dim(out, start, start + padded.shape[ax] - 2, axis=ax)
    return out


def advance(state_pad, velo_pad):
    state = window(state_pad, 0, 0)
    velo = window(velo_pad, 0, 0)
    advect = jnp.zeros_like(state)
    divergence = jnp.zeros_like(state[0])
    stretch = []
    for comp in range(3):
        axis = 3 - comp
        lower = window(state_pad, axis, -1)
        upper = window(state_pad, axis, 1)
        speed = velo[comp][None]
        advect = advect + jnp.maximum(speed, 0.0) * (state - lower) + jnp.minimum(speed, 0.0) * (upper - state)
        slope = 0.5 * (window(velo_pad, axis, 1) - window(velo_pad, axis, -1))
        divergence = divergence + slope[comp]
        stretch.append(state[0] * slope[0] + state[1] * slope[1] + state[2] * slope[2])
    moment = state[:3] - STEP_SIZE * (advect[:3] + jnp.stack(stretch) + state[:3] * divergence[None])
    image = state[3:] - STEP_SIZE * advect[3:]
    return jnp.concatenate([moment, image], axis=0)


def source(state, image_pad, target):
    residual_img = state[3] - target
    forces = []
    for comp in range(3):
        axis = 3 - comp
        slope = 0.5 * (window(image_pad, axis, 1) - window(image_pad, axis, -1))[0]
        forces.append(state[comp] - residual_img * slope)
    return jnp.stack(forces)


def reference(momentum, template, target):
    state = jnp.concatenate([momentum, template[None]], axis=0)
    for step in range(STEPS):
        velo = smooth(state[:3])
        state = advance(pad_one(state), pad_one(velo))
    image_pad = pad_one(state[3:])
    gradient = smooth(source(state, image_pad, target))
    return state[:3], state[3], gradient
```

```python
import jax
import jax.numpy as jnp
from jax import lax
from jax.sharding import PartitionSpec as P

STEPS = 2
TAPS = (0.05, 0.1, 0.2, 0.3, 0.2, 0.1, 0.05)
STEP_SIZE = 0.25
LANES = 128


def smooth_valid(f):
    width = f.shape[3]
    f = jnp.pad(f, ((0, 0), (0, 0), (0, 0), (3, 3)))
    for axis, length in ((3, width), (2, f.shape[2] - 6), (1, f.shape[1] - 6)):
        f = sum(TAPS[k] * lax.slice_in_dim(f, k, k + length, axis=axis) for k in range(7))
    return f


def shifted(f, axis, off):
    nd = f.ndim
    for back, ax in ((3, nd - 3), (2, nd - 2)):
        start = 1 + (off if back == axis else 0)
        f = lax.slice_in_dim(f, start, start + f.shape[ax] - 2, axis=ax)
    if axis == 1 and off:
        zero = jnp.zeros(f.shape[:-1] + (1,), f.dtype)
        if off > 0:
            f = jnp.concatenate([f[..., 1:], zero], axis=-1)
        else:
            f = jnp.concatenate([zero, f[..., :-1]], axis=-1)
    return f


def advect(v, f):
    mid = shifted(f, 0, 0)
    out = 0.0
    for comp in range(3):
        out = (
            out
            + jnp.maximum(v[comp], 0.0) * (mid - shifted(f, comp + 1, -1))
            + jnp.minimum(v[comp], 0.0) * (shifted(f, comp + 1, 1) - mid)
        )
    return out


def slope(f, comp):
    return 0.5 * (shifted(f, comp + 1, 1) - shifted(f, comp + 1, -1))


def advance_m(v, m):
    mid = shifted(m, 0, 0)
    vm = shifted(v, 0, 0)
    slopes = [slope(v, j) for j in range(3)]
    div = slopes[0][0] + slopes[1][1] + slopes[2][2]
    adv = advect(vm, m)
    stretch = jnp.stack([mid[0] * s[0] + mid[1] * s[1] + mid[2] * s[2] for s in slopes])
    return mid - STEP_SIZE * (adv + stretch + mid * div)


def rows_ext(cells, width, axis_name="gy"):
    dim = cells.ndim - 2
    count = lax.axis_size(axis_name)
    size = cells.shape[dim]
    head = lax.slice_in_dim(cells, 0, width, axis=dim)
    tail = lax.slice_in_dim(cells, size - width, size, axis=dim)
    up = lax.ppermute(tail, axis_name, [(i, i + 1) for i in range(count - 1)])
    down = lax.ppermute(head, axis_name, [(i + 1, i) for i in range(count - 1)])
    return jnp.concatenate([up, cells, down], axis=dim)


def on_device(momentum, template, target):
    n = lax.axis_size("gz")
    g = lax.axis_index("gz")
    p = lax.rem(g, 2)
    odd = p == 1
    rows, ny = lax.axis_index("gy"), lax.axis_size("gy")
    depth, height, full = template.shape
    half = full // 2
    wide = half + LANES

    def lanes(f, side):
        return lax.dynamic_slice_in_dim(f, side * (half - LANES), wide, axis=f.ndim - 1)

    swap = [(i, i ^ 1) for i in range(n)]
    up = [(i, i + 2) for i in range(n - 2)]
    down = [(i + 2, i) for i in range(n - 2)]
    outward = [(i, i + 2) if i % 2 else (i, i - 2) for i in range(n) if 0 <= (i + 2 if i % 2 else i - 2) < n]
    inward = [(i, i - 2) if i % 2 else (i, i + 2) for i in range(n) if 0 <= (i - 2 if i % 2 else i + 2) < n]

    def order(a, b):
        return jnp.where(odd, b, a), jnp.where(odd, a, b)

    m_own, i_own, t_own = (lanes(f, p) for f in (momentum, template, target))
    m_got = lax.ppermute(lanes(momentum, 1 - p), "gz", swap)
    m_out = lax.ppermute(m_own, "gz", outward)
    i_got = lax.ppermute(lanes(template, 1 - p), "gz", swap)
    i_out = lax.ppermute(lax.dynamic_slice_in_dim(i_own, (depth - 1) * p, 1, 0), "gz", outward)
    m_in = lax.ppermute(m_got, "gz", inward)
    i_in = lax.ppermute(lax.dynamic_slice_in_dim(i_got, (depth - 1) * (1 - p), 1, 0), "gz", inward)
    t_got = lax.ppermute(lanes(target, 1 - p), "gz", swap)
    below, above = order(m_in, m_out)
    low, high = order(m_own, m_got)
    m_ext = jnp.concatenate([below, low, high, above], axis=1)
    below, above = order(i_in, i_out)
    low, high = order(i_own, i_got)
    i_ext = jnp.concatenate([below, low, high, above], axis=0)
    targ = jnp.concatenate(order(t_own, t_got), axis=0)

    planes = 2 * depth
    zi = lax.broadcasted_iota(jnp.int32, (planes + 2, height + 2, 1), 0)
    yi = lax.broadcasted_iota(jnp.int32, (planes + 2, height + 2, 1), 1)
    slab = g // 2
    inside = ((zi > 0) | (slab > 0)) & ((zi < planes + 1) | (slab < n // 2 - 1))
    inside = inside & ((yi > 0) | (rows > 0)) & ((yi < height + 1) | (rows < ny - 1))

    for step in range(STEPS):
        last = step == STEPS - 1
        m_full = rows_ext(m_ext, 4)
        i_full = rows_ext(i_ext, 2 if last else 1)
        v = jnp.where(inside, smooth_valid(m_full), 0.0)
        m = advance_m(v, m_full[:, depth - 1 : depth + planes + 1, 3 : height + 5])
        if last:
            image = shifted(i_full, 0, 0) - STEP_SIZE * advect(v, i_full)
            image = jnp.where(inside, image, 0.0)
        else:
            image = shifted(i_full, 0, 0) - STEP_SIZE * advect(shifted(v, 0, 0), i_full)
            wd = 2 if step == STEPS - 2 else 1
            m_ext = jnp.concatenate(
                [lax.ppermute(m[:, -4:], "gz", up), m, lax.ppermute(m[:, :4], "gz", down)], axis=1
            )
            i_ext = jnp.concatenate(
                [lax.ppermute(image[-wd:], "gz", up), image, lax.ppermute(image[:wd], "gz", down)], axis=0
            )
    middle = shifted(image, 0, 0)
    q = jnp.stack([m[j] - (middle - targ) * slope(image, j) for j in range(3)])
    q = jnp.concatenate(
        [lax.ppermute(q[:, -3:], "gz", up), q, lax.ppermute(q[:, :3], "gz", down)], axis=1
    )

    def give_back(f):
        dim = f.ndim - 3
        f = lax.dynamic_slice_in_dim(f, LANES * p, half, axis=f.ndim - 1)
        kept = lax.dynamic_slice_in_dim(f, depth * p, depth, axis=dim)
        sent = lax.dynamic_slice_in_dim(f, depth * (1 - p), depth, axis=dim)
        return jnp.concatenate(order(kept, lax.ppermute(sent, "gz", swap)), axis=f.ndim - 1)

    m_res, i_res = give_back(m), give_back(middle)
    gradient = smooth_valid(rows_ext(q, 3))
    return m_res, i_res, give_back(gradient)


def solution(mesh):
    return jax.shard_map(
        on_device,
        mesh=mesh,
        in_specs=(
            P(None, ("groups", "gz"), "gy", None),
            P(("groups", "gz"), "gy", None),
            P(("groups", "gz"), "gy", None),
        ),
        out_specs=(
            P(None, ("groups", "gz"), "gy", None),
            P(("groups", "gz"), "gy", None),
            P(None, ("groups", "gz"), "gy", None),
        ),
        check_vma=False,
    )
```

```python
import functools

import jax
import jax.numpy as jnp
from jax import lax
from jax.experimental import pallas as pl
from jax.experimental.pallas import tpu as pltpu
from jax.sharding import PartitionSpec as P

STEPS = 2
TAPS = (0.05, 0.1, 0.2, 0.3, 0.2, 0.1, 0.05)
STEP_SIZE = 0.25
LANES = 128
SUB = 8


def taps7(load):
    return (
        TAPS[3] * load(0)
        + TAPS[2] * (load(-1) + load(1))
        + TAPS[1] * (load(-2) + load(2))
        + TAPS[0] * (load(-3) + load(3))
    )


def kernel(
    n, ny, half,
    m_hbm, i_hbm, t_hbm, mo_hbm, io_hbm, go_hbm,
    M0, M1, A, V, I0, I1, D, T, Q, M2, G,
    send_sem, recv_sem, loc_sem,
):
    g = lax.axis_index("gz")
    c = lax.axis_index("gy")
    p = lax.rem(g, 2)
    slab = lax.div(g, 2)
    nslab = n // 2
    partner = g + 1 - 2 * p
    depth = m_hbm.shape[1]
    planes = 2 * depth
    rows = m_hbm.shape[2]
    high = rows + 2 * SUB
    wide = half + LANES
    has_dn, has_up = slab > 0, slab < nslab - 1
    has_yl, has_yh = c > 0, c < ny - 1
    mid = slice(SUB, SUB + rows)

    count = [0, 0]

    def z_dev(d):
        return {"gz": d}

    def y_dev(d):
        return {"gy": d}

    class Copy:
        def __init__(self, src, dst, dev, sends=None, gets=None):
            k = count[0]
            count[0] += 1
            self.c = pltpu.make_async_remote_copy(
                src_ref=src, dst_ref=dst, send_sem=send_sem.at[k], recv_sem=recv_sem.at[k],
                device_id=dev, device_id_type=pl.DeviceIdType.MESH,
            )
            self.sends, self.gets = sends, gets

        def _do(self, cond, f):
            if cond is None:
                f()
            else:
                pl.when(cond)(f)

        def start(self):
            self._do(self.sends, self.c.start)
            return self

        def arrive(self):
            self._do(self.gets, self.c.wait_recv)

        def sent(self):
            self._do(self.sends, self.c.wait_send)

    def local(src, dst):
        k = count[1]
        count[1] += 1
        cp = pltpu.make_async_copy(src, dst, loc_sem.at[k])
        cp.start()
        return cp

    done = []

    barrier = pltpu.get_barrier_semaphore()

    def greet(dev):
        pl.semaphore_signal(barrier, inc=1, device_id=dev, device_id_type=pl.DeviceIdType.MESH)

    greet(z_dev(partner))
    for cond, dev in (
        (has_dn, z_dev(g - 2)), (has_up, z_dev(g + 2)), (has_yl, y_dev(c - 1)), (has_yh, y_dev(c + 1)),
    ):
        pl.when(cond)(functools.partial(greet, dev))
    friends = 1 + sum(jnp.where(cond, 1, 0) for cond in (has_dn, has_up, has_yl, has_yh))

    win = pl.multiple_of(p * (half - LANES), LANES)
    win_other = pl.multiple_of((1 - p) * (half - LANES), LANES)

    loc = [local(m_hbm.at[j, :, :, pl.ds(win, wide)], M0.at[j, pl.ds(4 + depth * p, depth), mid]) for j in range(3)]
    loc_i = local(i_hbm.at[:, :, pl.ds(win, wide)], I0.at[pl.ds(2 + depth * p, depth), mid])
    loc_t = local(t_hbm.at[:, :, pl.ds(win, wide)], T.at[pl.ds(depth * p, depth)])

    def blank(ref, *idx):
        ref[idx] = jnp.zeros(ref.at[idx].shape, jnp.float32)

    def blank_z(ref, lead, lo, hi):
        @pl.when(jnp.logical_not(has_dn))
        def _():
            blank(ref, *lead, slice(0, lo), mid)

        @pl.when(jnp.logical_not(has_up))
        def _():
            blank(ref, *lead, slice(hi, None), mid)

        @pl.when(jnp.logical_not(has_yl))
        def _():
            blank(ref, *lead, slice(None), slice(0, SUB))

        @pl.when(jnp.logical_not(has_yh))
        def _():
            blank(ref, *lead, slice(None), slice(SUB + rows, None))

    every = slice(None)
    pl.semaphore_wait(barrier, friends)

    out_dev = z_dev(g - 2 + 4 * p)
    in_dev = z_dev(g + 2 - 4 * p)
    odd = p == 1
    out_sends = jnp.logical_or(jnp.logical_and(odd, has_up), jnp.logical_and(p == 0, has_dn))
    out_gets = jnp.logical_or(jnp.logical_and(odd, has_dn), jnp.logical_and(p == 0, has_up))
    swaps, outs, ins = [], [], []
    for j in range(3):
        swaps.append(
            Copy(m_hbm.at[j, :, :, pl.ds(win_other, wide)], M0.at[j, pl.ds(4 + depth * p, depth), mid], z_dev(partner)).start()
        )
        outs.append(
            Copy(m_hbm.at[j, pl.ds((depth - 4) * p, 4), :, pl.ds(win, wide)], M0.at[j, pl.ds((planes + 4) * (1 - p), 4), mid], out_dev, out_sends, out_gets).start()
        )
    swap_i = Copy(i_hbm.at[:, :, pl.ds(win_other, wide)], I0.at[pl.ds(2 + depth * p, depth), mid], z_dev(partner)).start()
    out_i = Copy(
        i_hbm.at[pl.ds((depth - 1) * p, 1), :, pl.ds(win, wide)], I0.at[pl.ds(2 + planes - (planes + 1) * p, 1), mid], out_dev, out_sends, out_gets
    ).start()
    swap_t = Copy(t_hbm.at[:, :, pl.ds(win_other, wide)], T.at[pl.ds(depth * p, depth)], z_dev(partner)).start()

    blank_z(M0, (every,), 4, 4 + planes)
    blank_z(M1, (every,), 4, 4 + planes)
    blank_z(I0, (), 2, 2 + planes)
    blank_z(I1, (), 2, 2 + planes)
    blank_z(Q, (every,), 3, 3 + planes)

    def y_faces(view):
        lo = Copy(view(slice(SUB, 2 * SUB)), view(slice(SUB + rows, high)), y_dev(c - 1), has_yl, has_yh).start()
        hi = Copy(view(slice(rows, rows + SUB)), view(slice(0, SUB)), y_dev(c + 1), has_yh, has_yl).start()
        done.extend([lo, hi])
        return lo, hi

    for j in range(3):
        swaps[j].arrive()
        ins.append(
            Copy(
                M0.at[j, pl.ds(planes - (planes - 4) * p, 4), mid], M0.at[j, pl.ds((planes + 4) * p, 4), mid], in_dev, out_gets, out_sends
            ).start()
        )
    swap_i.arrive()
    in_i = Copy(
        I0.at[pl.ds(1 + planes - (planes - 1) * p, 1), mid], I0.at[pl.ds(1 + (planes + 1) * p, 1), mid], in_dev, out_gets, out_sends
    ).start()

    lane = lax.broadcasted_iota(jnp.int32, (SUB, wide), 1)
    keep = jnp.where(odd, lane, wide - 1 - lane) >= 3

    def keep_rows(r):
        return jnp.where(odd, lax.broadcasted_iota(jnp.int32, (r, wide), 1), wide - 1 - lax.broadcasted_iota(jnp.int32, (r, wide), 1)) >= 3

    def roll(f, s, axis):
        return pltpu.roll(f, s % f.shape[axis], axis)

    def smooth_xy(ref, j, depth_):
        def body(z, _):
            for t in range(high // SUB):
                f = jnp.where(keep, ref[j, z, t * SUB : (t + 1) * SUB], 0.0)
                A[j, z, t * SUB : (t + 1) * SUB] = taps7(lambda k: f if k == 0 else roll(f, -k, 1))
            f = A[j, z]
            for b in range(wide // LANES):
                s = f[:, b * LANES : (b + 1) * LANES]
                A[j, z, :, b * LANES : (b + 1) * LANES] = taps7(lambda k: s if k == 0 else roll(s, -k, 0))
            return 0

        lax.fori_loop(0, depth_, body, 0)

    zlast = planes + 1

    def outside(z, t, f):
        ok = jnp.logical_and(jnp.logical_or(z > 0, has_dn), jnp.logical_or(z < zlast, has_up))
        if t == 0:
            ok = jnp.logical_and(ok, has_yl)
        if t == high // SUB - 1:
            ok = jnp.logical_and(ok, has_yh)
        return f * jnp.where(ok, 1.0, 0.0)

    def smooth_z_velo(j):
        def body(z, _):
            for t in range(high // SUB):
                rs = slice(t * SUB, (t + 1) * SUB)
                f = taps7(lambda k: A[j, z + k + 3, rs])
                V[j, z, rs] = outside(z, t, jnp.where(keep, f, 0.0))
            return 0

        lax.fori_loop(0, planes + 2, body, 0)

    def around(load, z, t):
        lo, hi = max(0, (t - 1) * SUB), min(high, (t + 2) * SUB)
        tall = load(z, slice(lo, hi))
        at = slice(t * SUB - lo, t * SUB - lo + SUB)
        f = tall[at]
        rs = slice(t * SUB, (t + 1) * SUB)
        return f, (
            (roll(f, 1, 1), roll(f, -1, 1)),
            (roll(tall, 1, 0)[at], roll(tall, -1, 0)[at]),
            (load(z - 1, rs), load(z + 1, rs)),
        )

    def reader(ref, *lead):
        def load(z, rs):
            f = ref[(*lead, z, rs)]
            return jnp.where(keep_rows(f.shape[0]), f, 0.0)

        return load

    def plain(ref, *lead):
        return lambda z, rs: ref[(*lead, z, rs)]

    def advect(pos, neg, f, near):
        total = 0.0
        for i in range(3):
            total = total + pos[i] * (f - near[i][0]) + neg[i] * (near[i][1] - f)
        return total

    tiles = range(1, 1 + rows // SUB)

    def advance(Mi, zs, store):
        def body(z, _):
            for t in tiles:
                mids, nears = zip(*(around(reader(Mi, j), z + 4, t) for j in range(3)))
                v, vn = zip(*(around(plain(V, j), z + 1, t) for j in range(3)))
                pos = [jnp.maximum(u, 0.0) for u in v]
                neg = [jnp.minimum(u, 0.0) for u in v]
                div = 0.5 * sum(vn[i][i][1] - vn[i][i][0] for i in range(3))
                for j in range(3):
                    stretch = 0.5 * sum(mids[i] * (vn[i][j][1] - vn[i][j][0]) for i in range(3))
                    new = mids[j] - STEP_SIZE * (advect(pos, neg, mids[j], nears[j]) + stretch + mids[j] * div)
                    store(j, z, t, new)
            return 0

        lax.fori_loop(zs[0], zs[1], body, 0)

    def advance_image(Ii, z0, z1, ts, store):
        def body(z, _):
            for t in ts:
                f, near = around(reader(Ii), z + 1, t)
                v = [V[j, z, t * SUB : (t + 1) * SUB] for j in range(3)]
                pos = [jnp.maximum(u, 0.0) for u in v]
                neg = [jnp.minimum(u, 0.0) for u in v]
                store(z, t, f - STEP_SIZE * advect(pos, neg, f, near))
            return 0

        lax.fori_loop(z0, z1, body, 0)

    def tile(t):
        return slice(t * SUB, (t + 1) * SUB)

    for j in range(3):
        loc[j].wait()
        outs[j].arrive()
        ins[j].arrive()
        y_m = y_faces(lambda r: M0.at[j, :, r])
        if j == 0:
            loc_i.wait()
            out_i.arrive()
            in_i.arrive()
            y_i = y_faces(lambda r: I0.at[:, r])
        for f in y_m:
            f.arrive()
        smooth_xy(M0, j, planes + 8)
        smooth_z_velo(j)
    for f in y_i:
        f.arrive()

    def store_m1(j, z, t, f):
        M1[j, z + 4, tile(t)] = f

    def store_i1(z, t, f):
        I1[z + 1, tile(t)] = f

    dn, up = z_dev(g - 2), z_dev(g + 2)
    advance(M0, (0, 4), store_m1)
    go = [Copy(M1.at[j, 4:8, mid], M1.at[j, planes + 4 : planes + 8, mid], dn, has_dn, has_up).start() for j in range(3)]
    advance(M0, (planes - 4, planes), store_m1)
    gu = [Copy(M1.at[j, planes : planes + 4, mid], M1.at[j, 0:4, mid], up, has_up, has_dn).start() for j in range(3)]
    advance_image(I0, 1, planes + 1, tiles, store_i1)
    go_i = Copy(I1.at[2:4, mid], I1.at[planes + 2 : planes + 4, mid], dn, has_dn, has_up).start()
    gu_i = Copy(I1.at[planes : planes + 2, mid], I1.at[0:2, mid], up, has_up, has_dn).start()
    done.extend(swaps + outs + ins + [swap_i, out_i, in_i, swap_t] + go + gu + [go_i, gu_i])

    for j in range(3):
        go[j].arrive()
        gu[j].arrive()
        for f in y_faces(lambda r: M1.at[j, :, r]):
            f.arrive()
        smooth_xy(M1, j, planes + 8)
        smooth_z_velo(j)
    go_i.arrive()
    gu_i.arrive()
    y_i = y_faces(lambda r: I1.at[:, r])

    def store_m2(j, z, t, f):
        M2[j, z, (t - 1) * SUB : t * SUB] = f

    def store_i2(z, t, f):
        D[z, tile(t)] = outside(z, t, f)

    advance(M1, (0, planes), store_m2)
    for f in y_i:
        f.arrive()
    advance_image(I1, 0, planes + 2, range(high // SUB), store_i2)

    lanes_in = pl.ds(pl.multiple_of(LANES * p, LANES), half)
    lanes_out = pl.ds(pl.multiple_of(half * p, LANES), half)
    mine, theirs = pl.ds(depth * p, depth), pl.ds(depth * (1 - p), depth)
    locs = []

    def give(src, dst):
        done.append(Copy(src(theirs), dst, z_dev(partner)).start())
        locs.append(local(src(mine), dst))

    loc_t.wait()
    swap_t.arrive()

    def force(z0, z1):
        def body(z, _):
            for t in tiles:
                f, near = around(reader(D), z + 1, t)
                res = (f - T[z, (t - 1) * SUB : t * SUB]) * 0.5
                for j in range(3):
                    Q[j, z + 3, tile(t)] = M2[j, z, (t - 1) * SUB : t * SUB] - res * (near[j][1] - near[j][0])
            return 0

        lax.fori_loop(z0, z1, body, 0)

    force(0, 3)
    go = [Copy(Q.at[j, 3:6, mid], Q.at[j, planes + 3 : planes + 6, mid], dn, has_dn, has_up).start() for j in range(3)]
    force(planes - 3, planes)
    gu = [Copy(Q.at[j, planes : planes + 3, mid], Q.at[j, 0:3, mid], up, has_up, has_dn).start() for j in range(3)]
    force(3, planes - 3)
    done.extend(go + gu)
    for j in range(3):
        give(lambda z: M2.at[j, z, :, lanes_in], mo_hbm.at[j, :, :, lanes_out])

    def d_planes(z):
        return D.at[pl.ds(z.start + 1, depth), mid, lanes_in]

    give(d_planes, io_hbm.at[:, :, lanes_out])

    for j in range(3):
        go[j].arrive()
        gu[j].arrive()
        for f in y_faces(lambda r: Q.at[j, :, r]):
            f.arrive()
        smooth_xy(Q, j, planes + 6)

        def body(z, _):
            for t in tiles:
                G[j, z, (t - 1) * SUB : t * SUB] = taps7(lambda k: A[j, z + k + 3, tile(t)])
            return 0

        lax.fori_loop(0, planes, body, 0)
        give(lambda z: G.at[j, z, :, lanes_in], go_hbm.at[j, :, :, lanes_out])

    for f in done:
        f.sent()
    for f in done:
        if f.gets is None and f not in swaps and f is not swap_i and f is not swap_t:
            f.arrive()
    for f in locs:
        f.wait()


def solution(mesh):
    n, ny = mesh.shape["gz"], mesh.shape["gy"]

    def on_device(momentum, template, target):
        _, depth, rows, full = momentum.shape
        half = full // 2
        planes, high, wide = 2 * depth, rows + 2 * SUB, half + LANES

        def buf(*lead):
            return pltpu.VMEM((*lead, wide), jnp.float32)

        return pl.pallas_call(
            functools.partial(kernel, n, ny, half),
            out_shape=tuple(jax.ShapeDtypeStruct(a.shape, a.dtype) for a in (momentum, template, momentum)),
            in_specs=[pl.BlockSpec(memory_space=pl.ANY)] * 3,
            out_specs=[pl.BlockSpec(memory_space=pl.ANY)] * 3,
            scratch_shapes=[
                buf(3, planes + 8, high),
                buf(3, planes + 8, high),
                buf(3, planes + 8, high),
                buf(3, planes + 2, high),
                buf(planes + 4, high),
                buf(planes + 4, high),
                buf(planes + 2, high),
                buf(planes, rows),
                buf(3, planes + 6, high),
                buf(3, planes, rows),
                buf(3, planes, rows),
                pltpu.SemaphoreType.DMA((80,)),
                pltpu.SemaphoreType.DMA((80,)),
                pltpu.SemaphoreType.DMA((16,)),
            ],
            compiler_params=pltpu.CompilerParams(
                collective_id=0, has_side_effects=True, vmem_limit_bytes=56 * 1024 * 1024
            ),
        )(momentum, template, target)

    return jax.shard_map(
        on_device,
        mesh=mesh,
        in_specs=(
            P(None, ("groups", "gz"), "gy", None),
            P(("groups", "gz"), "gy", None),
            P(("groups", "gz"), "gy", None),
        ),
        out_specs=(
            P(None, ("groups", "gz"), "gy", None),
            P(("groups", "gz"), "gy", None),
            P(None, ("groups", "gz"), "gy", None),
        ),
        check_vma=False,
    )
```

```python
import functools

import jax
import jax.numpy as jnp
from jax import lax
from jax.experimental import pallas as pl
from jax.experimental.pallas import tpu as pltpu
from jax.sharding import PartitionSpec as P

STEPS = 2
TAPS = (0.05, 0.1, 0.2, 0.3, 0.2, 0.1, 0.05)
STEP_SIZE = 0.25
LANES = 128
SUB = 8


def taps7(load):
    return (
        TAPS[3] * load(0)
        + TAPS[2] * (load(-1) + load(1))
        + TAPS[1] * (load(-2) + load(2))
        + TAPS[0] * (load(-3) + load(3))
    )


def kernel(
    n, ny, half,
    m_hbm, i_hbm, t_hbm, mo_hbm, io_hbm, go_hbm,
    M0, M1, A, V, I0, I1, D, T, Q, M2, G,
    send_sem, recv_sem, loc_sem,
):
    g = lax.axis_index("gz")
    c = lax.axis_index("gy")
    p = lax.rem(g, 2)
    slab = lax.div(g, 2)
    nslab = n // 2
    partner = g + 1 - 2 * p
    depth = m_hbm.shape[1]
    planes = 2 * depth
    rows = m_hbm.shape[2]
    high = rows + 2 * SUB
    wide = half + LANES
    has_dn, has_up = slab > 0, slab < nslab - 1
    has_yl, has_yh = c > 0, c < ny - 1
    mid = slice(SUB, SUB + rows)

    count = [0, 0]

    def z_dev(d):
        return {"gz": d}

    def y_dev(d):
        return {"gy": d}

    class Copy:
        def __init__(self, src, dst, dev, sends=None, gets=None):
            k = count[0]
            count[0] += 1
            self.c = pltpu.make_async_remote_copy(
                src_ref=src, dst_ref=dst, send_sem=send_sem.at[k], recv_sem=recv_sem.at[k],
                device_id=dev, device_id_type=pl.DeviceIdType.MESH,
            )
            self.sends, self.gets = sends, gets

        def _do(self, cond, f):
            if cond is None:
                f()
            else:
                pl.when(cond)(f)

        def start(self):
            self._do(self.sends, self.c.start)
            return self

        def arrive(self):
            self._do(self.gets, self.c.wait_recv)

        def sent(self):
            self._do(self.sends, self.c.wait_send)

    def local(src, dst):
        k = count[1]
        count[1] += 1
        cp = pltpu.make_async_copy(src, dst, loc_sem.at[k])
        cp.start()
        return cp

    done = []

    barrier = pltpu.get_barrier_semaphore()

    def greet(dev):
        pl.semaphore_signal(barrier, inc=1, device_id=dev, device_id_type=pl.DeviceIdType.MESH)

    greet(z_dev(partner))
    for cond, dev in (
        (has_dn, z_dev(g - 2)), (has_up, z_dev(g + 2)), (has_yl, y_dev(c - 1)), (has_yh, y_dev(c + 1)),
    ):
        pl.when(cond)(functools.partial(greet, dev))
    friends = 1 + sum(jnp.where(cond, 1, 0) for cond in (has_dn, has_up, has_yl, has_yh))

    win = pl.multiple_of(p * (half - LANES), LANES)
    win_other = pl.multiple_of((1 - p) * (half - LANES), LANES)

    loc = [local(m_hbm.at[j, :, :, pl.ds(win, wide)], M0.at[j, pl.ds(4 + depth * p, depth), mid]) for j in range(3)]
    loc_i = local(i_hbm.at[:, :, pl.ds(win, wide)], I0.at[pl.ds(2 + depth * p, depth), mid])
    loc_t = local(t_hbm.at[:, :, pl.ds(win, wide)], T.at[pl.ds(depth * p, depth)])

    def blank(ref, *idx):
        ref[idx] = jnp.zeros(ref.at[idx].shape, jnp.float32)

    def blank_z(ref, lead, lo, hi):
        @pl.when(jnp.logical_not(has_dn))
        def _():
            blank(ref, *lead, slice(0, lo), mid)

        @pl.when(jnp.logical_not(has_up))
        def _():
            blank(ref, *lead, slice(hi, None), mid)

        @pl.when(jnp.logical_not(has_yl))
        def _():
            blank(ref, *lead, slice(None), slice(0, SUB))

        @pl.when(jnp.logical_not(has_yh))
        def _():
            blank(ref, *lead, slice(None), slice(SUB + rows, None))

    every = slice(None)
    pl.semaphore_wait(barrier, friends)

    out_dev = z_dev(g - 2 + 4 * p)
    in_dev = z_dev(g + 2 - 4 * p)
    odd = p == 1
    out_sends = jnp.logical_or(jnp.logical_and(odd, has_up), jnp.logical_and(p == 0, has_dn))
    out_gets = jnp.logical_or(jnp.logical_and(odd, has_dn), jnp.logical_and(p == 0, has_up))
    swaps, outs, ins = [], [], []
    for j in range(3):
        swaps.append(
            Copy(m_hbm.at[j, :, :, pl.ds(win_other, wide)], M0.at[j, pl.ds(4 + depth * p, depth), mid], z_dev(partner)).start()
        )
        outs.append(
            Copy(m_hbm.at[j, pl.ds((depth - 4) * p, 4), :, pl.ds(win, wide)], M0.at[j, pl.ds((planes + 4) * (1 - p), 4), mid], out_dev, out_sends, out_gets).start()
        )
    swap_i = Copy(i_hbm.at[:, :, pl.ds(win_other, wide)], I0.at[pl.ds(2 + depth * p, depth), mid], z_dev(partner))
    out_i = Copy(
        i_hbm.at[pl.ds((depth - 1) * p, 1), :, pl.ds(win, wide)], I0.at[pl.ds(2 + planes - (planes + 1) * p, 1), mid], out_dev, out_sends, out_gets
    ).start()
    swap_t = Copy(t_hbm.at[:, :, pl.ds(win_other, wide)], T.at[pl.ds(depth * p, depth)], z_dev(partner))

    blank_z(M0, (every,), 4, 4 + planes)
    blank_z(M1, (every,), 4, 4 + planes)
    blank_z(I0, (), 2, 2 + planes)
    blank_z(I1, (), 2, 2 + planes)
    blank_z(Q, (every,), 3, 3 + planes)

    def y_faces(view):
        lo = Copy(view(slice(SUB, 2 * SUB)), view(slice(SUB + rows, high)), y_dev(c - 1), has_yl, has_yh).start()
        hi = Copy(view(slice(rows, rows + SUB)), view(slice(0, SUB)), y_dev(c + 1), has_yh, has_yl).start()
        done.extend([lo, hi])
        return lo, hi

    for j in range(3):
        swaps[j].arrive()
        ins.append(
            Copy(
                M0.at[j, pl.ds(planes - (planes - 4) * p, 4), mid], M0.at[j, pl.ds((planes + 4) * p, 4), mid], in_dev, out_gets, out_sends
            ).start()
        )
    swap_i.start()
    in_i = Copy(
        I0.at[pl.ds(1 + planes - (planes - 1) * p, 1), mid], I0.at[pl.ds(1 + (planes + 1) * p, 1), mid], in_dev, out_gets, out_sends
    )

    lane = lax.broadcasted_iota(jnp.int32, (SUB, wide), 1)
    keep = jnp.where(odd, lane, wide - 1 - lane) >= 3

    def keep_rows(r):
        return jnp.where(odd, lax.broadcasted_iota(jnp.int32, (r, wide), 1), wide - 1 - lax.broadcasted_iota(jnp.int32, (r, wide), 1)) >= 3

    keep_all = keep_rows(high)

    def roll(f, s, axis):
        return pltpu.roll(f, s % f.shape[axis], axis)

    def taps_cyclic(f, axis):
        u = 2.0 * f + (roll(f, 1, axis) + roll(f, -1, axis))
        return TAPS[0] * (3.0 * u + (roll(u, 2, axis) + roll(u, -2, axis)))

    def smooth(ref, j, depth_, store):
        def body(z, _):
            for t in range(high // SUB):
                rs = slice(t * SUB, (t + 1) * SUB)
                f = jnp.where(keep, taps7(lambda k: ref[j, z + k + 3, rs]), 0.0)
                A[rs] = taps_cyclic(f, 1)
            for b in range(wide // LANES):
                ls = slice(b * LANES, (b + 1) * LANES)
                store(z, ls, taps_cyclic(A[:, ls], 0))
            return 0

        lax.fori_loop(0, depth_, body, 0)

    zlast = planes + 1

    def outside(z, t, f):
        ok = jnp.logical_and(jnp.logical_or(z > 0, has_dn), jnp.logical_or(z < zlast, has_up))
        if t == 0:
            ok = jnp.logical_and(ok, has_yl)
        if t == high // SUB - 1:
            ok = jnp.logical_and(ok, has_yh)
        return f * jnp.where(ok, 1.0, 0.0)

    row = lax.broadcasted_iota(jnp.int32, (high, LANES), 0)

    def smooth_velo(ref, j):
        def store(z, ls, f):
            ok = jnp.logical_and(jnp.logical_or(z > 0, has_dn), jnp.logical_or(z < zlast, has_up))
            lo = jnp.where(has_yl, 0, SUB)
            hi = jnp.where(ok, jnp.where(has_yh, high, SUB + rows), 0)
            inside = jnp.logical_and(row >= lo, row < hi)
            if ls.start == 0 or ls.stop == wide:
                inside = jnp.logical_and(inside, keep_all[:, ls])
            V[j, z, :, ls] = jnp.where(inside, f, 0.0)

        smooth(ref, j, planes + 2, store)

    def around(load, z, t):
        lo, hi = max(0, (t - 1) * SUB), min(high, (t + 2) * SUB)
        tall = load(z, slice(lo, hi))
        at = slice(t * SUB - lo, t * SUB - lo + SUB)
        f = tall[at]
        rs = slice(t * SUB, (t + 1) * SUB)
        return f, (
            (roll(f, 1, 1), roll(f, -1, 1)),
            (roll(tall, 1, 0)[at], roll(tall, -1, 0)[at]),
            (load(z - 1, rs), load(z + 1, rs)),
        )

    def reader(ref, *lead):
        def load(z, rs):
            f = ref[(*lead, z, rs)]
            return jnp.where(keep_rows(f.shape[0]), f, 0.0)

        return load

    def plain(ref, *lead):
        return lambda z, rs: ref[(*lead, z, rs)]

    def advect(pos, neg, f, near):
        total = 0.0
        for i in range(3):
            total = total + pos[i] * (f - near[i][0]) + neg[i] * (near[i][1] - f)
        return total

    tiles = range(1, 1 + rows // SUB)

    def advance(Mi, zs, store):
        def body(z, _):
            for t in tiles:
                mids, nears = zip(*(around(reader(Mi, j), z + 4, t) for j in range(3)))
                v, vn = zip(*(around(plain(V, j), z + 1, t) for j in range(3)))
                pos = [jnp.maximum(u, 0.0) for u in v]
                neg = [jnp.minimum(u, 0.0) for u in v]
                div = 0.5 * sum(vn[i][i][1] - vn[i][i][0] for i in range(3))
                for j in range(3):
                    stretch = 0.5 * sum(mids[i] * (vn[i][j][1] - vn[i][j][0]) for i in range(3))
                    new = mids[j] - STEP_SIZE * (advect(pos, neg, mids[j], nears[j]) + stretch + mids[j] * div)
                    store(j, z, t, new)
            return 0

        lax.fori_loop(zs[0], zs[1], body, 0)

    def advance_image(Ii, z0, z1, ts, store):
        def body(z, _):
            for t in ts:
                f, near = around(reader(Ii), z + 1, t)
                v = [V[j, z, t * SUB : (t + 1) * SUB] for j in range(3)]
                pos = [jnp.maximum(u, 0.0) for u in v]
                neg = [jnp.minimum(u, 0.0) for u in v]
                store(z, t, f - STEP_SIZE * advect(pos, neg, f, near))
            return 0

        lax.fori_loop(z0, z1, body, 0)

    def tile(t):
        return slice(t * SUB, (t + 1) * SUB)

    for j in range(3):
        loc[j].wait()
        outs[j].arrive()
        ins[j].arrive()
        for f in y_faces(lambda r: M0.at[j, :, r]):
            f.arrive()
        smooth_velo(M0, j)
        if j == 0:
            swap_i.arrive()
            in_i.start()
            swap_t.start()
    loc_i.wait()
    out_i.arrive()
    in_i.arrive()
    y_i = y_faces(lambda r: I0.at[:, r])

    def store_m1(j, z, t, f):
        M1[j, z + 4, tile(t)] = f

    def store_i1(z, t, f):
        I1[z + 1, tile(t)] = f

    dn, up = z_dev(g - 2), z_dev(g + 2)
    advance(M0, (0, 4), store_m1)
    go = [Copy(M1.at[j, 4:8, mid], M1.at[j, planes + 4 : planes + 8, mid], dn, has_dn, has_up).start() for j in range(3)]
    advance(M0, (planes - 4, planes), store_m1)
    gu = [Copy(M1.at[j, planes : planes + 4, mid], M1.at[j, 0:4, mid], up, has_up, has_dn).start() for j in range(3)]
    own = [y_faces(lambda r: M1.at[j, 4 : 4 + planes, r]) for j in range(3)]
    for f in y_i:
        f.arrive()
    advance_image(I0, 1, planes + 1, tiles, store_i1)
    go_i = Copy(I1.at[2:4, mid], I1.at[planes + 2 : planes + 4, mid], dn, has_dn, has_up).start()
    gu_i = Copy(I1.at[planes : planes + 2, mid], I1.at[0:2, mid], up, has_up, has_dn).start()
    done.extend(swaps + outs + ins + [swap_i, out_i, in_i, swap_t] + go + gu + [go_i, gu_i])

    for j in range(3):
        go[j].arrive()
        gu[j].arrive()
        ends = y_faces(lambda r: M1.at[j, 0:4, r]) + y_faces(lambda r: M1.at[j, 4 + planes : 8 + planes, r])
        for f in own[j] + ends:
            f.arrive()
        smooth_velo(M1, j)
    go_i.arrive()
    gu_i.arrive()
    y_i = y_faces(lambda r: I1.at[:, r])

    def store_m2(j, z, t, f):
        M2[j, z, (t - 1) * SUB : t * SUB] = f

    def store_i2(z, t, f):
        D[z, tile(t)] = outside(z, t, f)

    lanes_in = pl.ds(pl.multiple_of(LANES * p, LANES), half)
    lanes_out = pl.ds(pl.multiple_of(half * p, LANES), half)
    mine, theirs = pl.ds(depth * p, depth), pl.ds(depth * (1 - p), depth)
    locs = []

    def give(src, dst):
        done.append(Copy(src(theirs), dst, z_dev(partner)).start())
        locs.append(local(src(mine), dst))

    def d_planes(z):
        return D.at[pl.ds(z.start + 1, depth), mid, lanes_in]

    advance(M1, (0, planes), store_m2)
    for j in range(3):
        give(lambda z: M2.at[j, z, :, lanes_in], mo_hbm.at[j, :, :, lanes_out])
    for f in y_i:
        f.arrive()
    advance_image(I1, 0, planes + 2, range(high // SUB), store_i2)

    loc_t.wait()
    swap_t.arrive()

    def force(z0, z1):
        def body(z, _):
            for t in tiles:
                f, near = around(reader(D), z + 1, t)
                res = (f - T[z, (t - 1) * SUB : t * SUB]) * 0.5
                for j in range(3):
                    Q[j, z + 3, tile(t)] = M2[j, z, (t - 1) * SUB : t * SUB] - res * (near[j][1] - near[j][0])
            return 0

        lax.fori_loop(z0, z1, body, 0)

    force(0, 3)
    go = [Copy(Q.at[j, 3:6, mid], Q.at[j, planes + 3 : planes + 6, mid], dn, has_dn, has_up).start() for j in range(3)]
    force(planes - 3, planes)
    gu = [Copy(Q.at[j, planes : planes + 3, mid], Q.at[j, 0:3, mid], up, has_up, has_dn).start() for j in range(3)]
    force(3, planes - 3)
    own = [y_faces(lambda r: Q.at[j, 3 : 3 + planes, r]) for j in range(3)]
    done.extend(go + gu)
    give(d_planes, io_hbm.at[:, :, lanes_out])

    for j in range(3):
        go[j].arrive()
        gu[j].arrive()
        ends = y_faces(lambda r: Q.at[j, 0:3, r]) + y_faces(lambda r: Q.at[j, 3 + planes : 6 + planes, r])
        for f in own[j] + ends:
            f.arrive()

        def store_g(z, ls, f):
            G[j, z, :, ls] = f[mid]

        smooth(Q, j, planes, store_g)
        give(lambda z: G.at[j, z, :, lanes_in], go_hbm.at[j, :, :, lanes_out])

    for f in done:
        f.sent()
    for f in done:
        if f.gets is None and f not in swaps and f is not swap_i and f is not swap_t:
            f.arrive()
    for f in locs:
        f.wait()


def solution(mesh):
    n, ny = mesh.shape["gz"], mesh.shape["gy"]

    def on_device(momentum, template, target):
        _, depth, rows, full = momentum.shape
        half = full // 2
        planes, high, wide = 2 * depth, rows + 2 * SUB, half + LANES

        def buf(*lead):
            return pltpu.VMEM((*lead, wide), jnp.float32)

        return pl.pallas_call(
            functools.partial(kernel, n, ny, half),
            out_shape=tuple(jax.ShapeDtypeStruct(a.shape, a.dtype) for a in (momentum, template, momentum)),
            in_specs=[pl.BlockSpec(memory_space=pl.ANY)] * 3,
            out_specs=[pl.BlockSpec(memory_space=pl.ANY)] * 3,
            scratch_shapes=[
                buf(3, planes + 8, high),
                buf(3, planes + 8, high),
                buf(high),
                buf(3, planes + 2, high),
                buf(planes + 4, high),
                buf(planes + 4, high),
                buf(planes + 2, high),
                buf(planes, rows),
                buf(3, planes + 6, high),
                buf(3, planes, rows),
                buf(3, planes, rows),
                pltpu.SemaphoreType.DMA((96,)),
                pltpu.SemaphoreType.DMA((96,)),
                pltpu.SemaphoreType.DMA((16,)),
            ],
            compiler_params=pltpu.CompilerParams(
                collective_id=0, has_side_effects=True, vmem_limit_bytes=56 * 1024 * 1024
            ),
        )(momentum, template, target)

    return jax.shard_map(
        on_device,
        mesh=mesh,
        in_specs=(
            P(None, ("groups", "gz"), "gy", None),
            P(("groups", "gz"), "gy", None),
            P(("groups", "gz"), "gy", None),
        ),
        out_specs=(
            P(None, ("groups", "gz"), "gy", None),
            P(("groups", "gz"), "gy", None),
            P(None, ("groups", "gz"), "gy", None),
        ),
        check_vma=False,
    )
```
